128 devices in a mesh: slab: 32 (over y, z, core), mode: 4 (over x).
Axes of the slice: x: 4, y: 4, z: 4, core: 2. Of those that a mesh axis runs over, the one named last changes fastest.
Arguments:
- mode_shapes: bfloat16 [32768, 256], P('slab', 'mode'), may hold values from -6 to 6
- stiffness: bfloat16 [49152, 128, 128], P(('slab', 'mode'))
- elem_block: int32 [49152], P(('slab', 'mode')), may hold values from 0 to 15
- touched: int32 [32, 24], P('slab'), may hold values from 0 to 63, as said below
Outputs:
- coupling: float32 [64, 256, 256], P('slab', None, 'mode')
- sensitivity: float32 [64, 256], P('slab', 'mode')
The draws below stay inside these ranges and needn't reach their ends.
Inputs may be any that keep to these rules, and one draw needn't show every extreme that they name: Every parameter is owned by slab parameter // 2; in each row of touched the 24 parameters have distinct owners, and row s holds one parameter owned by slab s.
All inputs are finite; a program needn't handle non-finite values.
Results may differ from the reference program's by a relative error of at most 0.0029.
Values may be sent and summed in bfloat16 or wider, within the bound.
No kernel may reach another device: no remote copies, remote signals or barrier semaphores. Data moves between devices by JAX's collectives and lax.ppermute only.
A program may use at most 128 MiB of HBM per device.

```python
import jax
import jax.numpy as jnp
from jax import lax

MODES = 256
BLOCK = 64
ROWS_DEV = 1024
P_DEV = 2
G_DEV = 24
EL_GRP = 16
SLABS = 32
DOFS = 32768
PARAMS = 64
ELEMS = 49152
N_MODE = 4


def draw_stiffness(key, part):
    key = jax.random.fold_in(key, 11)
    width_dofs = 2 * BLOCK
    factor = 1.0 / (width_dofs * EL_GRP ** 0.5)
    noise = jax.random.normal(key, (ELEMS, width_dofs, width_dofs), jnp.float32)
    return (noise * factor).astype(jnp.bfloat16)


def draw_touched(key, part):
    key = jax.random.fold_in(key, 23)

    def one_row(layer_position):
        row_key = jax.random.fold_in(key, layer_position)
        others = 1 + jax.random.permutation(row_key, SLABS - 1)[:G_DEV - 1]
        offsets = jnp.concatenate([jnp.zeros((1,), jnp.int32), others.astype(jnp.int32)])
        owners = (layer_position + offsets) % SLABS
        subs = jax.random.randint(jax.random.fold_in(row_key, 1), (G_DEV,), 0, P_DEV).astype(jnp.int32)
        subs = subs.at[0].set(layer_position % P_DEV)
        return owners * P_DEV + subs
    return jax.vmap(one_row)(jnp.arange(SLABS, dtype=jnp.int32)).astype(jnp.int32)


def with_ends(drawn, stream_key, low, high):
    longest = drawn.shape.index(max(drawn.shape))
    spots = []
    for shift in (0, 1):
        where = [jax.random.randint(jax.random.fold_in(stream_key, axis), (), 0, length) for axis, length in enumerate(drawn.shape)]
        where[longest] = (where[longest] + shift) % drawn.shape[longest]
        spots.append(tuple(where))
    return drawn.at[spots[0]].set(low).at[spots[1]].set(high)


def level_of(rng, dims, pieces, least, high):
    factor_of, own = 1.0, jax.random.fold_in(rng, 6)
    for dim, shards_of in pieces:
        heights = jnp.exp(jax.random.uniform(jax.random.fold_in(own, dim), (shards_of,), jnp.float32, least / len(pieces), high / len(pieces)))
        factor_of = factor_of * jnp.repeat(heights, dims[dim] // shards_of).reshape([-1 if axis == dim else 1 for axis in range(len(dims))])
    return factor_of


def scatter_about(stream_key, shape, width, limit, pieces=(), held_as=jnp.bfloat16):
    factor_of = level_of(stream_key, shape, pieces, -0.22, 0.18) if pieces else 1.0
    result = jax.random.normal(stream_key, shape, jnp.float32) * width * factor_of
    return jnp.minimum(jnp.maximum(result, -limit), limit).astype(held_as)


def setup_inputs(seed: int = 0) -> dict:
    seeds = jax.random.split(jax.random.key(seed), 5)
    mode_shapes = scatter_about(seeds[0], (DOFS, MODES), 1.0, 6.0, ((0, 32), (1, 4)))
    stiffness = draw_stiffness(jax.random.fold_in(seeds[4], 71), 0)
    elem_block = with_ends(jax.random.randint(seeds[2], (ELEMS,), 0, ROWS_DEV // BLOCK), jax.random.fold_in(seeds[2], 1), 0, (ROWS_DEV // BLOCK) - 1).astype(jnp.int32)
    touched = draw_touched(jax.random.fold_in(seeds[4], 71), 0)
    return dict(mode_shapes=mode_shapes, stiffness=stiffness, elem_block=elem_block, touched=touched)


def reference(mode_shapes, stiffness, elem_block, touched):
    member_freedoms = 2 * BLOCK
    padded = jnp.concatenate([mode_shapes, jnp.zeros((BLOCK, MODES), mode_shapes.dtype)], 0)
    line_strips = padded.reshape(DOFS // BLOCK + 1, BLOCK, MODES)
    rigidity_matrices = stiffness.reshape(SLABS * N_MODE, G_DEV, EL_GRP, member_freedoms, member_freedoms)
    blocks_all = elem_block.reshape(SLABS * N_MODE, G_DEV, EL_GRP).astype(jnp.int32)

    def one_device(running_total, device_idx):
        layer_position = device_idx // N_MODE
        stiffness_local = rigidity_matrices[device_idx]
        block_dev = blocks_all[device_idx] + layer_position * (ROWS_DEV // BLOCK)

        def one_group(pair):
            stiff_group, block_group = pair
            shapes = jnp.concatenate([line_strips[block_group], line_strips[block_group + 1]], axis=1)
            shapes = shapes.astype(jnp.float32)
            images = jnp.einsum('ers,esm->erm', stiff_group.astype(jnp.float32), shapes)
            images = lax.optimization_barrier(images.astype(jnp.bfloat16)).astype(jnp.float32)
            return jnp.einsum('erm,ern->mn', shapes, images)

        partial_value = lax.map(one_group, (stiffness_local, block_dev))
        return running_total.at[touched[layer_position]].add(partial_value), None

    start = jnp.zeros((PARAMS, MODES, MODES), jnp.float32)
    coupling, unused = lax.scan(one_device, start, jnp.arange(SLABS * N_MODE, dtype=jnp.int32))
    sensitivity = jnp.diagonal(coupling, axis1=1, axis2=2)
    return coupling, sensitivity
```

```python
import jax
import jax.numpy as jnp
from jax import lax
from jax.experimental import pallas as pl
from jax.experimental.pallas import tpu as pltpu
from jax.sharding import PartitionSpec as P

BLK = 64
STRIPS = 16
GROUPS = 24
PER_GROUP = 16
STEP = 4
SLOTS = 32
HALF = 128
MODES = 256


def coupling_kernel(block_ref, slot_ref, mode_ref, pieces, next_pieces, stiff, out, shapes, shapes_t):
    step = pl.program_id(0)

    @pl.when(step == 0)
    def _():
        out[...] = jnp.zeros_like(out)
        for t in range(2):
            for k in range(2):
                shapes[0:1024, 128 * t + 64 * k:128 * t + 64 * k + 64] = pieces[2 * t + k][...]
                shapes[1024:1088, 128 * t + 64 * k:128 * t + 64 * k + 64] = next_pieces[2 * t + k][...]
        for k in range(4):
            place = pl.multiple_of(lax.rem(mode_ref[0] + 4 - k, 4) * 64, 64)
            for b in range(STRIPS):
                shapes_t[b, pl.ds(place, 64), :] = shapes[b * BLK:b * BLK + 128, 64 * k:64 * k + 64].T

    low = lax.broadcasted_iota(jnp.int32, (HALF, HALF), 1) < 64
    for g in range(STEP):
        lefts, images = [], []
        for e in range(PER_GROUP):
            b = block_ref[(step * STEP + g) * PER_GROUP + e]
            x = shapes[pl.ds(pl.multiple_of(b * BLK, BLK), 128), :]
            y = jnp.dot(stiff[g * PER_GROUP + e], x, preferred_element_type=jnp.float32)
            images.append(y.astype(jnp.bfloat16))
            lefts.append(shapes_t[b])
        c = jnp.dot(jnp.concatenate(lefts, 1), jnp.concatenate(images, 0), preferred_element_type=jnp.float32)
        slot = slot_ref[step * STEP + g]
        for t in range(2):
            top, bottom = c[:HALF, 128 * t:128 * t + 128], c[HALF:, 128 * t:128 * t + 128]
            even = jnp.where(low, top, pltpu.roll(bottom, 64, 1))
            odd = jnp.where(low, pltpu.roll(top, 64, 1), bottom)
            out[slot, lax.rem(mode_ref[0] + 4 - 2 * t, 4)] = even.astype(jnp.bfloat16)
            out[slot, lax.rem(mode_ref[0] + 3 - 2 * t, 4)] = odd.astype(jnp.bfloat16)


def coupling_blocks(pieces, next_pieces, stiffness, elem_block, slots, mode):
    def body(block_ref, slot_ref, mode_ref, *refs):
        coupling_kernel(block_ref, slot_ref, mode_ref, refs[0:4], refs[4:8], *refs[8:])

    whole = lambda shape: pl.BlockSpec(shape, lambda i, *_: (0,) * len(shape))
    return pl.pallas_call(
        body,
        name="coupling_blocks",
        out_shape=jax.ShapeDtypeStruct((SLOTS, 4, HALF, HALF), jnp.bfloat16),
        grid_spec=pltpu.PrefetchScalarGridSpec(
            num_scalar_prefetch=3,
            grid=(GROUPS // STEP,),
            in_specs=[whole((1024, 64))] * 4 + [whole((64, 64))] * 4
            + [pl.BlockSpec((STEP * PER_GROUP, 128, 128), lambda i, *_: (i, 0, 0))],
            out_specs=whole((SLOTS, 4, HALF, HALF)),
            scratch_shapes=[
                pltpu.VMEM((1088, MODES), jnp.bfloat16),
                pltpu.VMEM((STRIPS, MODES, 128), jnp.bfloat16),
            ],
        ),
        compiler_params=pltpu.CompilerParams(vmem_limit_bytes=48 * 2**20),
        cost_estimate=pl.CostEstimate(flops=9663676416, bytes_accessed=18 * 2**20, transcendentals=0),
    )(elem_block, slots, mode, *pieces, *next_pieces, stiffness)


def owner_sum_kernel(sub_ref, mode_ref, got, coupling, sens, total):
    total[...] = jnp.zeros_like(total)

    def one_slab(s, carry):
        sub = sub_ref[s]

        @pl.when(sub >= 0)
        def _():
            part = got[4 * s].astype(jnp.float32)
            for x in range(1, 4):
                part += got[4 * s + x].astype(jnp.float32)
            total[sub] += part

        return carry

    lax.fori_loop(0, SLOTS, one_slab, 0)
    row = lax.broadcasted_iota(jnp.int32, (HALF, 64), 0)
    col = lax.broadcasted_iota(jnp.int32, (HALF, 64), 1)
    own = col + 64 * mode_ref[0]
    for p in range(2):
        top, bottom = total[p][:, :64], total[p][:, 64:]
        coupling[p, :HALF, :] = top
        coupling[p, HALF:, :] = bottom
        diagonal = jnp.where(row == own, top, 0.0) + jnp.where(row + HALF == own, bottom, 0.0)
        sens[p:p + 1, :] = jnp.sum(diagonal, axis=0, keepdims=True)


def owner_sum(sub, mode, got):
    return pl.pallas_call(
        owner_sum_kernel,
        name="owner_sum",
        out_shape=(
            jax.ShapeDtypeStruct((2, MODES, 64), jnp.float32),
            jax.ShapeDtypeStruct((2, 64), jnp.float32),
        ),
        in_specs=[pl.BlockSpec(memory_space=pltpu.SMEM)] * 2 + [pl.BlockSpec(memory_space=pltpu.VMEM)],
        out_specs=[pl.BlockSpec(memory_space=pltpu.VMEM)] * 2,
        scratch_shapes=[pltpu.VMEM((2, HALF, HALF), jnp.float32)],
        compiler_params=pltpu.CompilerParams(vmem_limit_bytes=32 * 2**20),
    )(sub, mode, got)


def per_device(mode_shapes, stiffness, elem_block, touched):
    modes = lax.axis_size("mode")
    slabs = lax.axis_size("slab")
    mode = lax.axis_index("mode").astype(jnp.int32)
    slab = lax.axis_index("slab").astype(jnp.int32)
    next_own = lax.ppermute(mode_shapes[:BLK], "slab", [(i, i - 1) for i in range(1, slabs)])
    around = lambda k: [(i, (i + k) % modes) for i in range(modes)]
    pieces = [mode_shapes] + [lax.ppermute(mode_shapes, "mode", around(k)) for k in (1, 2, 3)]
    next_pieces = [next_own] + [lax.ppermute(next_own, "mode", around(k)) for k in (1, 2, 3)]
    slots = touched[0] // 2
    hit = slots[None, :] == jnp.arange(slabs, dtype=jnp.int32)[:, None]
    sub = jnp.max(jnp.where(hit, touched[0][None, :] % 2, -1), axis=1)
    subs = lax.all_to_all(jnp.broadcast_to(sub[:, None, None], (slabs, 1, 128)), "slab", 0, 0, tiled=True)[:, 0, 0]
    out = coupling_blocks(pieces, next_pieces, stiffness, elem_block, slots, mode[None])
    got = lax.all_to_all(out.reshape(slabs * modes, HALF, HALF), ("slab", "mode"), 0, 0, tiled=True)
    return tuple(owner_sum(subs, mode[None], got))


def solution(mesh):
    return jax.shard_map(
        per_device,
        mesh=mesh,
        in_specs=(
            P("slab", "mode"),
            P(("slab", "mode"), None, None),
            P(("slab", "mode")),
            P("slab", None),
        ),
        out_specs=(P("slab", None, "mode"), P("slab", "mode")),
        check_vma=False,
    )
```

```python
import jax
import jax.numpy as jnp
from jax import lax
from jax.experimental import pallas as pl
from jax.experimental.pallas import tpu as pltpu
from jax.sharding import PartitionSpec as P

BLK = 64
STRIPS = 16
GROUPS = 24
PER_GROUP = 16
STEP = 4
SLOTS = 32
HALF = 128
MODES = 256
SF = 48
MF = HALF - SF
SF_ROWS = 4 * SF + 16
VMEM = pl.BlockSpec(memory_space=pltpu.VMEM)
SMEM = pl.BlockSpec(memory_space=pltpu.SMEM)


def whole(shape):
    return pl.BlockSpec(shape, lambda i, *_: (0,) * len(shape))


def shape_of(*dims, dtype=jnp.bfloat16):
    return jax.ShapeDtypeStruct(dims, dtype)


def coupling_kernel(block_ref, touched_ref, mode_ref, *refs):
    pieces, next_pieces, stiff, slab_first = refs[0:4], refs[4:8], refs[8], refs[9]
    mode_first, shapes, shapes_t = refs[10:14], refs[14], refs[15]
    step = pl.program_id(0)

    @pl.when(step == 0)
    def _():
        slab_first[...] = jnp.zeros_like(slab_first)
        for r in range(8):
            rows = [piece[:, 128 * r:128 * r + 128] for piece in pieces]
            shapes[128 * r:128 * r + 128, :] = jnp.concatenate(rows, 0).T
        beyond = jnp.concatenate([piece[...] for piece in next_pieces], 0)
        shapes[1024:1088, :] = beyond.T[:BLK]
        for k in range(4):
            place = pl.multiple_of(lax.rem(mode_ref[0] + 4 - k, 4) * 64, 64)
            for b in range(STRIPS):
                if b % 2 == 0:
                    strip = pieces[k][:, BLK * b:BLK * b + 128]
                elif b < STRIPS - 1:
                    strip = pieces[k][:, BLK * b:BLK * b + 128]
                else:
                    strip = jnp.concatenate([pieces[k][:, BLK * b:], next_pieces[k][:, :BLK]], 1)
                shapes_t[b, pl.ds(place, 64), :] = strip

    low = lax.broadcasted_iota(jnp.int32, (HALF, HALF), 1) < 64
    for g in range(STEP):
        lefts, images = [], []
        for e in range(PER_GROUP):
            b = block_ref[(step * STEP + g) * PER_GROUP + e]
            x = shapes[pl.ds(pl.multiple_of(b * BLK, BLK), 128), :]
            y = jnp.dot(stiff[g * PER_GROUP + e], x, preferred_element_type=jnp.float32)
            images.append(y.astype(jnp.bfloat16))
            lefts.append(shapes_t[b])
        c = jnp.dot(jnp.concatenate(lefts, 1), jnp.concatenate(images, 0), preferred_element_type=jnp.float32)
        param = touched_ref[step * STEP + g]
        slot = lax.shift_right_logical(param, 1)
        flag = (param & 1).astype(jnp.float32) + 1.0
        slab_first[slot, 4 * SF:, :] = jnp.full((16, HALF), flag, jnp.float32).astype(jnp.bfloat16)
        for t in range(2):
            top, bottom = c[:HALF, 128 * t:128 * t + 128], c[HALF:, 128 * t:128 * t + 128]
            even = jnp.where(low, top, pltpu.roll(bottom, 64, 1))
            odd = jnp.where(low, pltpu.roll(top, 64, 1), bottom)
            for k, block in ((2 * t, even), (2 * t + 1, odd)):
                slab_first[slot, SF * k:SF * k + SF, :] = block[:SF].astype(jnp.bfloat16)
                mode_first[k][g] = block[SF:].astype(mode_first[k].dtype)


def coupling_blocks(pieces, next_pieces, stiffness, elem_block, touched, mode):
    return pl.pallas_call(
        coupling_kernel,
        name="coupling_blocks",
        out_shape=[shape_of(SLOTS, SF_ROWS, HALF), shape_of(GROUPS, MF, HALF, dtype=jnp.float32)]
        + [shape_of(GROUPS, MF, HALF)] * 3,
        grid_spec=pltpu.PrefetchScalarGridSpec(
            num_scalar_prefetch=3,
            grid=(GROUPS // STEP,),
            in_specs=[whole((64, 1024))] * 4 + [whole((64, 128))] * 4
            + [pl.BlockSpec((STEP * PER_GROUP, 128, 128), lambda i, *_: (i, 0, 0))],
            out_specs=[whole((SLOTS, SF_ROWS, HALF))]
            + [pl.BlockSpec((STEP, MF, HALF), lambda i, *_: (i, 0, 0))] * 4,
            scratch_shapes=[
                pltpu.VMEM((1088, MODES), jnp.bfloat16),
                pltpu.VMEM((STRIPS, MODES, 128), jnp.bfloat16),
            ],
        ),
        compiler_params=pltpu.CompilerParams(vmem_limit_bytes=48 * 2**20),
        cost_estimate=pl.CostEstimate(flops=9663676416, bytes_accessed=18 * 2**20, transcendentals=0),
    )(elem_block, touched, mode, *pieces, *next_pieces, stiffness)


def slab_sum_kernel(got, own, *rest):
    outs, flags = (own,) + rest[:3], rest[3]
    for k in range(4):
        sums = [jnp.zeros((SF, HALF), jnp.float32)] * 2
        for s in range(SLOTS):
            flag = got[s, 4 * SF:, :].astype(jnp.float32)[:1]
            block = got[s, SF * k:SF * k + SF, :].astype(jnp.float32)
            sums = [sums[p] + jnp.where(flag == p + 1.0, block, 0.0) for p in range(2)]
        for p in range(2):
            outs[k][p] = sums[p]
    for s in range(SLOTS):
        flags[s] = got[s, 4 * SF:, :].astype(jnp.float32)[:8]


def slab_sum(got):
    return pl.pallas_call(
        slab_sum_kernel,
        name="slab_sum",
        out_shape=[shape_of(2, SF, HALF, dtype=jnp.float32)] * 4 + [shape_of(SLOTS, 8, HALF, dtype=jnp.float32)],
        in_specs=[VMEM],
        out_specs=[VMEM] * 5,
        cost_estimate=pl.CostEstimate(flops=2**22, bytes_accessed=2**21, transcendentals=0),
    )(got)


def mode_sum_kernel(touched_ref, own, a, b, c, out):
    out[...] = jnp.zeros_like(out)
    for g in range(GROUPS):
        total = own[g] + a[g].astype(jnp.float32) + b[g].astype(jnp.float32) + c[g].astype(jnp.float32)
        out[lax.shift_right_logical(touched_ref[g], 1)] = total.astype(jnp.bfloat16)


def mode_sum(touched, own, got):
    return pl.pallas_call(
        mode_sum_kernel,
        name="mode_sum",
        out_shape=shape_of(SLOTS, MF, HALF),
        in_specs=[SMEM] + [VMEM] * 4,
        out_specs=VMEM,
        cost_estimate=pl.CostEstimate(flops=2**20, bytes_accessed=3 * 2**20, transcendentals=0),
    )(touched, own, *got)


def final_kernel(mode_ref, got, flags, own, a, b, c, coupling, sens):
    sums = [jnp.zeros((MF, HALF), jnp.float32)] * 2
    for s in range(SLOTS):
        block = got[s].astype(jnp.float32)
        sums = [sums[p] + jnp.where(flags[s, :1, :] == p + 1.0, block, 0.0) for p in range(2)]
    row = lax.broadcasted_iota(jnp.int32, (HALF, HALF), 0)
    lane = lax.broadcasted_iota(jnp.int32, (HALF, HALF), 1)
    on_diagonal = jnp.where(lane < 64, row, row + 192) == lane + 64 * mode_ref[0]
    for p in range(2):
        packed = jnp.concatenate([own[p] + a[p] + b[p] + c[p], sums[p]], 0)
        columns = packed.T
        coupling[p, :, :HALF] = columns[:64]
        coupling[p, :, HALF:] = columns[64:]
        diagonal = jnp.sum(jnp.where(on_diagonal, packed, 0.0), axis=0, keepdims=True)
        sens[p:p + 1, :] = diagonal[:, :64] + diagonal[:, 64:]


def final_sum(mode, got, flags, own, tails):
    return pl.pallas_call(
        final_kernel,
        name="final_sum",
        out_shape=(shape_of(2, 64, MODES, dtype=jnp.float32), shape_of(2, 64, dtype=jnp.float32)),
        in_specs=[SMEM] + [VMEM] * 6,
        out_specs=[VMEM] * 2,
    )(mode, got, flags, own, *tails)


def per_device(mode_shapes, stiffness, elem_block, touched):
    modes = lax.axis_size("mode")
    slabs = lax.axis_size("slab")
    mode = lax.axis_index("mode").astype(jnp.int32)[None]
    params = touched[0]
    around = lambda k: [(i, (i + k) % modes) for i in range(modes)]
    own = mode_shapes.T
    next_own = lax.ppermute(own[:, :HALF], "slab", [(i, i - 1) for i in range(1, slabs)])
    pieces = [own] + [lax.ppermute(own, "mode", around(k)) for k in (1, 3, 2)]
    pieces = [pieces[0], pieces[1], pieces[3], pieces[2]]
    next_pieces = [next_own] + [lax.ppermute(next_own, "mode", around(k)) for k in (1, 2, 3)]
    slab_first, own_first, *mode_first = coupling_blocks(
        pieces, next_pieces, stiffness, elem_block, params, mode)
    crossed = [lax.ppermute(mode_first[k - 1], "mode", around(-k)) for k in (1, 2, 3)]
    got = lax.all_to_all(slab_first, "slab", 0, 0, tiled=True)
    tail_own, t1, t2, t3, flags = slab_sum(got)
    tails = [lax.ppermute(t, "mode", around(-k)) for k, t in ((1, t1), (2, t2), (3, t3))]
    rows = lax.all_to_all(mode_sum(params, own_first, crossed), "slab", 0, 0, tiled=True)
    coupling, sensitivity = final_sum(mode, rows, flags, tail_own, tails)
    return jnp.swapaxes(coupling, 1, 2), sensitivity


def solution(mesh):
    return jax.shard_map(
        per_device,
        mesh=mesh,
        in_specs=(
            P("slab", "mode"),
            P(("slab", "mode"), None, None),
            P(("slab", "mode")),
            P("slab", None),
        ),
        out_specs=(P("slab", None, "mode"), P("slab", "mode")),
        check_vma=False,
    )
```

```python
import jax
import jax.numpy as jnp
from jax import lax
from jax.experimental import pallas as pl
from jax.experimental.pallas import tpu as pltpu
from jax.sharding import PartitionSpec as P

BLK = 64
STRIPS = 16
PARTS = (8, 16)
GROUPS = sum(PARTS)
PER_GROUP = 16
STEPS = 2
SLOTS = 32
HALF = 128
MODES = 256
SF = 48
MF = HALF - SF
FLAG_AT = 4 * SF
SF_ROWS = FLAG_AT + 16
TOUCHED_AT = GROUPS * PER_GROUP
MODE_AT = TOUCHED_AT + GROUPS
SHAPES = (1088, MODES)
SHAPES_T = (STRIPS, MODES, 128)
VMEM = pl.BlockSpec(memory_space=pltpu.VMEM)
SMEM = pl.BlockSpec(memory_space=pltpu.SMEM)
HBM = pl.BlockSpec(memory_space=pltpu.HBM)


def shape_of(*dims, dtype=jnp.bfloat16):
    return jax.ShapeDtypeStruct(dims, dtype)


def limit(mib):
    return pltpu.CompilerParams(vmem_limit_bytes=mib * 2**20)


def load_kernel(stiff, loaded, sems):
    size = stiff.shape[0] // 8
    copies = [pltpu.make_async_copy(stiff.at[pl.ds(i * size, size)], loaded.at[pl.ds(i * size, size)], sems.at[i])
              for i in range(8)]
    for copy in copies:
        copy.start()
    for copy in copies:
        copy.wait()


def load_stiffness(stiffness):
    return pl.pallas_call(
        load_kernel,
        name="load_stiffness",
        out_shape=shape_of(*stiffness.shape),
        in_specs=[HBM],
        out_specs=VMEM,
        scratch_shapes=[pltpu.SemaphoreType.DMA((8,))],
        compiler_params=limit(16),
        cost_estimate=pl.CostEstimate(flops=0, bytes_accessed=2 * stiffness.size, transcendentals=0),
    )(pltpu.with_memory_space_constraint(stiffness, pltpu.HBM))


def prepare(mode, pieces, shapes, shapes_t):
    for r in range(9):
        rows = jnp.concatenate([piece[:, 128 * r:128 * r + 128] for piece in pieces], 0).T
        if r < 8:
            shapes[128 * r:128 * r + 128, :] = rows
        else:
            shapes[1024:1088, :] = rows[:BLK]
    for k in range(4):
        place = pl.multiple_of(lax.rem(mode + 4 - k, 4) * 64, 64)
        for b in range(STRIPS):
            shapes_t[b, pl.ds(place, 64), :] = pieces[k][:, BLK * b:BLK * b + 128]


def coupling_groups(first, groups, ints, stiff, shapes, shapes_t, slab_row, mode_first):
    low = lax.broadcasted_iota(jnp.int32, (HALF, HALF), 1) < 64

    def one_group(g):
        lefts, images = [], []
        for e in range(PER_GROUP):
            b = ints[(first + g) * PER_GROUP + e]
            x = shapes[pl.ds(pl.multiple_of(b * BLK, BLK), 128), :]
            y = jnp.dot(stiff[(first + g) * PER_GROUP + e], x, preferred_element_type=jnp.float32)
            images.append(y.astype(jnp.bfloat16))
            lefts.append(shapes_t[b])
        c = jnp.dot(jnp.concatenate(lefts, 1), jnp.concatenate(images, 0), preferred_element_type=jnp.float32)
        ref, at = slab_row(g)
        flag = (ints[TOUCHED_AT + first + g] & 1).astype(jnp.float32) + 1.0
        ref[at, FLAG_AT:, :] = jnp.full((16, HALF), flag, jnp.float32).astype(jnp.bfloat16)
        for t in range(2):
            top, bottom = c[:HALF, 128 * t:128 * t + 128], c[HALF:, 128 * t:128 * t + 128]
            even = jnp.where(low, top, pltpu.roll(bottom, 64, 1))
            odd = jnp.where(low, pltpu.roll(top, 64, 1), bottom)
            for k, block in ((2 * t, even), (2 * t + 1, odd)):
                ref[at, SF * k:SF * k + SF, :] = block[:SF].astype(jnp.bfloat16)
                mode_first[k][g] = block[SF:].astype(jnp.bfloat16)

    def one_step(j, carry):
        for h in range(groups // STEPS):
            one_group(j * (groups // STEPS) + h)
        return carry

    lax.fori_loop(0, STEPS, one_step, 0)


def slot_of(ints, group):
    return lax.shift_right_logical(ints[TOUCHED_AT + group], 1)


def first_kernel(ints, p0, p3, p2, p1, stiff, rows, own, a, b, c, shapes, shapes_t):
    prepare(ints[MODE_AT], (p0, p1, p2, p3), shapes, shapes_t)
    coupling_groups(0, PARTS[0], ints, stiff, shapes, shapes_t, lambda g: (rows, g), (own, a, b, c))


def second_kernel(ints, shapes, shapes_t, stiff, before, slab_first, own, a, b, c):
    slab_first[...] = jnp.zeros_like(slab_first)
    for g in range(PARTS[0]):
        slab_first[slot_of(ints, g)] = before[g]
    coupling_groups(PARTS[0], PARTS[1], ints, stiff, shapes, shapes_t,
                    lambda g: (slab_first, slot_of(ints, PARTS[0] + g)), (own, a, b, c))


def coupling_call(kernel, name, groups, rows, args, more_outs=()):
    return pl.pallas_call(
        kernel,
        name=name,
        out_shape=[shape_of(rows, SF_ROWS, HALF)] + [shape_of(groups, MF, HALF)] * 4
        + [shape_of(*dims) for dims in more_outs],
        in_specs=[SMEM] + [VMEM] * (len(args) - 1),
        out_specs=[VMEM] * (5 + len(more_outs)),
        compiler_params=limit(16),
        cost_estimate=pl.CostEstimate(
            flops=groups * 402653184, bytes_accessed=groups * 2**20, transcendentals=0),
    )(*args)


def slab_sum_kernel(got, own, a, b, c, flags):
    for k, out in enumerate((own, a, b, c)):
        sums = [jnp.zeros((SF, HALF), jnp.float32)] * 2
        for s in range(SLOTS):
            flag = got[s, FLAG_AT:, :].astype(jnp.float32)[:1]
            block = got[s, SF * k:SF * k + SF, :].astype(jnp.float32)
            sums = [sums[p] + jnp.where(flag == p + 1.0, block, 0.0) for p in range(2)]
        for p in range(2):
            out[p] = sums[p]
    for s in range(SLOTS):
        flags[s] = got[s, FLAG_AT:, :].astype(jnp.float32)[:8]


def slab_sum(got):
    return pl.pallas_call(
        slab_sum_kernel,
        name="slab_sum",
        out_shape=[shape_of(2, SF, HALF, dtype=jnp.float32)] * 4 + [shape_of(SLOTS, 8, HALF, dtype=jnp.float32)],
        in_specs=[VMEM],
        out_specs=[VMEM] * 5,
        compiler_params=limit(12),
        cost_estimate=pl.CostEstimate(flops=2**22, bytes_accessed=2**21, transcendentals=0),
    )(got)


def mode_sum_kernel(ints, *refs):
    out = refs[-1]
    out[...] = jnp.zeros_like(out)
    for part, groups in enumerate(PARTS):
        own, a, b, c = refs[4 * part:4 * part + 4]
        for g in range(groups):
            total = own[g].astype(jnp.float32) + a[g].astype(jnp.float32) + b[g].astype(jnp.float32) + c[g].astype(jnp.float32)
            out[slot_of(ints, sum(PARTS[:part]) + g)] = total.astype(jnp.bfloat16)


def mode_sum(ints, parts):
    return pl.pallas_call(
        mode_sum_kernel,
        name="mode_sum",
        out_shape=shape_of(SLOTS, MF, HALF),
        in_specs=[SMEM] + [VMEM] * (4 * len(PARTS)),
        out_specs=VMEM,
        compiler_params=limit(12),
        cost_estimate=pl.CostEstimate(flops=2**20, bytes_accessed=3 * 2**20, transcendentals=0),
    )(ints, *[array for part in parts for array in part])


def final_kernel(ints, got, flags, own, a, b, c, coupling, sens):
    row = lax.broadcasted_iota(jnp.int32, (HALF, HALF), 0)
    lane = lax.broadcasted_iota(jnp.int32, (HALF, HALF), 1)
    on_diagonal = jnp.where(lane < 64, row, row + 192) == lane + 64 * ints[MODE_AT]
    sums = [jnp.zeros((MF, HALF), jnp.float32)] * 2
    for s in range(SLOTS):
        block = got[s].astype(jnp.float32)
        sums = [sums[p] + jnp.where(flags[s, :1, :] == p + 1.0, block, 0.0) for p in range(2)]
    for p in range(2):
        packed = jnp.concatenate([own[p] + a[p] + b[p] + c[p], sums[p]], 0)
        columns = packed.T
        coupling[p, :, :HALF] = columns[:64]
        coupling[p, :, HALF:] = columns[64:]
        diagonal = jnp.sum(jnp.where(on_diagonal, packed, 0.0), axis=0, keepdims=True)
        sens[p:p + 1, :] = diagonal[:, :64] + diagonal[:, 64:]


def final_sum(ints, got, flags, own, tails):
    return pl.pallas_call(
        final_kernel,
        name="final_sum",
        out_shape=(shape_of(2, 64, MODES, dtype=jnp.float32), shape_of(2, 64, dtype=jnp.float32)),
        in_specs=[SMEM] + [VMEM] * 6,
        out_specs=[VMEM] * 2,
        compiler_params=limit(12),
    )(ints, got, flags, own, *tails)


def per_device(mode_shapes, stiffness, elem_block, touched):
    modes = lax.axis_size("mode")
    slabs = lax.axis_size("slab")
    mode = lax.axis_index("mode").astype(jnp.int32)[None]
    around = lambda k: [(i, (i + k) % modes) for i in range(modes)]
    own = mode_shapes.T
    next_own = lax.ppermute(own[:, :HALF], "slab", [(i, i - 1) for i in range(1, slabs)])
    ints = jnp.concatenate([elem_block, touched[0], mode])
    own, ints = lax.optimization_barrier((jnp.concatenate([own, next_own], 1), ints))
    one, three, two = [lax.ppermute(own, "mode", around(k)) for k in (1, 3, 2)]
    loaded = load_stiffness(stiffness)
    rows, *part_a, shapes, shapes_t = coupling_call(
        first_kernel, "coupling_a", PARTS[0], PARTS[0], (ints, own, three, two, one, loaded), [SHAPES, SHAPES_T])
    crossed_a = [lax.ppermute(part_a[k], "mode", around(-k)) for k in (1, 2, 3)]
    slab_first, *part_b = coupling_call(
        second_kernel, "coupling_b", PARTS[1], SLOTS, (ints, shapes, shapes_t, loaded, rows))
    crossed_b = [lax.ppermute(part_b[k], "mode", around(-k)) for k in (1, 2, 3)]
    slab_first, crossed_a = lax.optimization_barrier((slab_first, crossed_a))
    got = lax.all_to_all(slab_first, "slab", 0, 0, tiled=True)
    tail_own, t1, t2, t3, flags = slab_sum(got)
    tails = [lax.ppermute(t, "mode", around(-k)) for k, t in ((1, t1), (2, t2), (3, t3))]
    summed = mode_sum(ints, [part_a[:1] + crossed_a, part_b[:1] + crossed_b])
    later = lax.all_to_all(summed, "slab", 0, 0, tiled=True)
    coupling, sensitivity = final_sum(ints, later, flags, tail_own, tails)
    return jnp.swapaxes(coupling, 1, 2), sensitivity


def solution(mesh):
    return jax.shard_map(
        per_device,
        mesh=mesh,
        in_specs=(
            P("slab", "mode"),
            P(("slab", "mode"), None, None),
            P(("slab", "mode")),
            P("slab", None),
        ),
        out_specs=(P("slab", None, "mode"), P("slab", "mode")),
        check_vma=False,
    )
```

```python
import jax
import jax.numpy as jnp
from jax import lax
from jax.experimental import pallas as pl
from jax.experimental.pallas import tpu as pltpu
from jax.sharding import PartitionSpec as P

BLK = 64
STRIPS = 16
PARTS = (12, 12)
GROUPS = sum(PARTS)
PER_GROUP = 16
STEPS = 1
SLOTS = 32
HALF = 128
MODES = 256
FLAG_ROWS = 16
TOUCHED_AT = GROUPS * PER_GROUP
MODE_AT = TOUCHED_AT + GROUPS
SHAPES = (1088, MODES)
SHAPES_T = (STRIPS, MODES, 128)
VMEM = pl.BlockSpec(memory_space=pltpu.VMEM)
SUM_WEIGHT = 2 * 10**10
SMEM = pl.BlockSpec(memory_space=pltpu.SMEM)
HBM = pl.BlockSpec(memory_space=pltpu.HBM)


def shape_of(*dims, dtype=jnp.bfloat16):
    return jax.ShapeDtypeStruct(dims, dtype)


def limit(mib):
    return pltpu.CompilerParams(vmem_limit_bytes=mib * 2**20)


def load_kernel(stiff, loaded, sems):
    size = stiff.shape[0] // 8
    copies = [pltpu.make_async_copy(stiff.at[pl.ds(i * size, size)], loaded.at[pl.ds(i * size, size)], sems.at[i])
              for i in range(8)]
    for copy in copies:
        copy.start()
    for copy in copies:
        copy.wait()


def load_stiffness(stiffness):
    return pl.pallas_call(
        load_kernel,
        name="load_stiffness",
        out_shape=shape_of(*stiffness.shape),
        in_specs=[HBM],
        out_specs=VMEM,
        scratch_shapes=[pltpu.SemaphoreType.DMA((8,))],
        compiler_params=limit(16),
        cost_estimate=pl.CostEstimate(flops=0, bytes_accessed=2 * stiffness.size, transcendentals=0),
    )(pltpu.with_memory_space_constraint(stiffness, pltpu.HBM))


def prepare(mode, pieces, shapes, shapes_t):
    for r in range(9):
        rows = jnp.concatenate([piece[:, 128 * r:128 * r + 128] for piece in pieces], 0).T
        if r < 8:
            shapes[128 * r:128 * r + 128, :] = rows
        else:
            shapes[1024:1088, :] = rows[:BLK]
    for k in range(4):
        place = pl.multiple_of(lax.rem(mode + 4 - k, 4) * 64, 64)
        for b in range(STRIPS):
            shapes_t[b, pl.ds(place, 64), :] = pieces[k][:, BLK * b:BLK * b + 128]


def coupling_groups(first, groups, ints, stiff, shapes, shapes_t, slab_row, mode_first):
    low = lax.broadcasted_iota(jnp.int32, (HALF, HALF), 1) < 64

    def one_group(g):
        lefts, images = [], []
        for e in range(PER_GROUP):
            b = ints[(first + g) * PER_GROUP + e]
            x = shapes[pl.ds(pl.multiple_of(b * BLK, BLK), 128), :]
            y = jnp.dot(stiff[(first + g) * PER_GROUP + e], x, preferred_element_type=jnp.float32)
            images.append(y.astype(jnp.bfloat16))
            lefts.append(shapes_t[b])
        c = jnp.dot(jnp.concatenate(lefts, 1), jnp.concatenate(images, 0), preferred_element_type=jnp.float32)
        ref, at = slab_row(g)
        flag = (ints[TOUCHED_AT + first + g] & 1).astype(jnp.float32) + 1.0
        ref[at, HALF:, :] = jnp.full((FLAG_ROWS, HALF), flag, jnp.float32).astype(jnp.bfloat16)
        for t in range(2):
            top, bottom = c[:HALF, 128 * t:128 * t + 128], c[HALF:, 128 * t:128 * t + 128]
            even = jnp.where(low, top, pltpu.roll(bottom, 64, 1)).astype(jnp.bfloat16)
            odd = jnp.where(low, pltpu.roll(top, 64, 1), bottom).astype(jnp.bfloat16)
            if t == 0:
                mode_first[0][g] = even
            else:
                ref[at, :HALF, :] = even
            mode_first[t + 1][g] = odd

    def one_step(j, carry):
        for h in range(groups // STEPS):
            one_group(j * (groups // STEPS) + h)
        return carry

    lax.fori_loop(0, STEPS, one_step, 0)


def slot_of(ints, group):
    return lax.shift_right_logical(ints[TOUCHED_AT + group], 1)


def first_kernel(ints, p0, p3, p2, p1, stiff, rows, own, a, b, shapes, shapes_t):
    prepare(ints[MODE_AT], (p0, p1, p2, p3), shapes, shapes_t)
    coupling_groups(0, PARTS[0], ints, stiff, shapes, shapes_t, lambda g: (rows, g), (own, a, b))


def second_kernel(ints, shapes, shapes_t, stiff, before, slab_first, own, a, b):
    slab_first[...] = jnp.zeros_like(slab_first)
    for g in range(PARTS[0]):
        slab_first[slot_of(ints, g)] = before[g]
    coupling_groups(PARTS[0], PARTS[1], ints, stiff, shapes, shapes_t,
                    lambda g: (slab_first, slot_of(ints, PARTS[0] + g)), (own, a, b))


def coupling_call(kernel, name, groups, rows, args, more_outs=()):
    return pl.pallas_call(
        kernel,
        name=name,
        out_shape=[shape_of(rows, HALF + FLAG_ROWS, HALF)] + [shape_of(groups, HALF, HALF)] * 3
        + [shape_of(*dims) for dims in more_outs],
        in_specs=[SMEM] + [VMEM] * (len(args) - 1),
        out_specs=[VMEM] * (4 + len(more_outs)),
        compiler_params=limit(16),
        cost_estimate=pl.CostEstimate(
            flops=groups * 402653184, bytes_accessed=groups * 2**20, transcendentals=0),
    )(*args)


def sum_of_slabs(got, flag_of):
    sums = [jnp.zeros((HALF, HALF), jnp.float32)] * 2
    for s in range(SLOTS):
        block = got[s, :HALF, :].astype(jnp.float32)
        sums = [sums[p] + jnp.where(flag_of(s) == p + 1.0, block, 0.0) for p in range(2)]
    return sums


def slab_sum_kernel(got, out, flags):
    for s in range(SLOTS):
        flags[s] = got[s, HALF:, :].astype(jnp.float32)[:8]
    for p, total in enumerate(sum_of_slabs(got, lambda s: got[s, HALF:, :].astype(jnp.float32)[:1])):
        out[p] = total


def slab_sum(got):
    return pl.pallas_call(
        slab_sum_kernel,
        name="slab_sum",
        out_shape=[shape_of(2, HALF, HALF, dtype=jnp.float32), shape_of(SLOTS, 8, HALF, dtype=jnp.float32)],
        in_specs=[VMEM],
        out_specs=[VMEM] * 2,
        compiler_params=limit(12),
        cost_estimate=pl.CostEstimate(flops=2**22, bytes_accessed=2**21, transcendentals=0),
    )(got)


def mode_sum_kernel(ints, *refs):
    out = refs[-1]
    out[...] = jnp.zeros_like(out)
    for part, groups in enumerate(PARTS):
        for g in range(groups):
            own, a, b = [ref[g].astype(jnp.float32) for ref in refs[3 * part:3 * part + 3]]
            out[slot_of(ints, sum(PARTS[:part]) + g)] = (own + a + b).astype(jnp.bfloat16)


def mode_sum(ints, parts):
    return pl.pallas_call(
        mode_sum_kernel,
        name="mode_sum",
        out_shape=shape_of(SLOTS, HALF, HALF),
        in_specs=[SMEM] + [VMEM] * (3 * len(PARTS)),
        out_specs=VMEM,
        compiler_params=limit(12),
        cost_estimate=pl.CostEstimate(flops=SUM_WEIGHT, bytes_accessed=3 * 2**20, transcendentals=0),
    )(ints, *[array for part in parts for array in part])


def final_kernel(ints, got, flags, tail, coupling, sens):
    row = lax.broadcasted_iota(jnp.int32, (HALF, HALF), 0)
    lane = lax.broadcasted_iota(jnp.int32, (HALF, HALF), 1)
    on_diagonal = jnp.where(lane < 64, row, row + 192) == lane + 64 * ints[MODE_AT]
    for p, total in enumerate(sum_of_slabs(got, lambda s: flags[s, :1, :])):
        packed = total + tail[p]
        columns = packed.T
        coupling[p, :, :HALF] = columns[:64]
        coupling[p, :, HALF:] = columns[64:]
        diagonal = jnp.sum(jnp.where(on_diagonal, packed, 0.0), axis=0, keepdims=True)
        sens[p:p + 1, :] = diagonal[:, :64] + diagonal[:, 64:]


def final_sum(ints, got, flags, tail):
    return pl.pallas_call(
        final_kernel,
        name="final_sum",
        out_shape=(shape_of(2, 64, MODES, dtype=jnp.float32), shape_of(2, 64, dtype=jnp.float32)),
        in_specs=[SMEM] + [VMEM] * 3,
        out_specs=[VMEM] * 2,
        compiler_params=limit(12),
    )(ints, got, flags, tail)


def per_device(mode_shapes, stiffness, elem_block, touched):
    modes = lax.axis_size("mode")
    slabs = lax.axis_size("slab")
    mode = lax.axis_index("mode").astype(jnp.int32)[None]
    around = lambda k: [(i, (i + k) % modes) for i in range(modes)]
    own = mode_shapes.T
    next_own = lax.ppermute(own[:, :HALF], "slab", [(i, i - 1) for i in range(1, slabs)])
    ints = jnp.concatenate([elem_block, touched[0], mode])
    own, ints = lax.optimization_barrier((jnp.concatenate([own, next_own], 1), ints))
    one, three, two = [lax.ppermute(own, "mode", around(k)) for k in (1, 3, 2)]
    loaded = load_stiffness(stiffness)
    rows, *part_a, shapes, shapes_t = coupling_call(
        first_kernel, "coupling_a", PARTS[0], PARTS[0], (ints, own, three, two, one, loaded), [SHAPES, SHAPES_T])
    crossed_a = [lax.ppermute(part_a[1], "mode", around(-1)), lax.ppermute(part_a[2], "mode", around(1))]
    slab_first, *part_b = coupling_call(
        second_kernel, "coupling_b", PARTS[1], SLOTS, (ints, shapes, shapes_t, loaded, rows))
    crossed_b = [lax.ppermute(part_b[1], "mode", around(-1)), lax.ppermute(part_b[2], "mode", around(1))]
    slab_first, crossed_a = lax.optimization_barrier((slab_first, crossed_a))
    got = lax.all_to_all(slab_first, "slab", 0, 0, tiled=True)
    two_away, flags = slab_sum(got)
    tail = lax.ppermute(two_away, "mode", around(-2))
    summed = mode_sum(ints, [part_a[:1] + crossed_a, part_b[:1] + crossed_b])
    later = lax.all_to_all(summed, "slab", 0, 0, tiled=True)
    coupling, sensitivity = final_sum(ints, later, flags, tail)
    return jnp.swapaxes(coupling, 1, 2), sensitivity


def solution(mesh):
    return jax.shard_map(
        per_device,
        mesh=mesh,
        in_specs=(
            P("slab", "mode"),
            P(("slab", "mode"), None, None),
            P(("slab", "mode")),
            P("slab", None),
        ),
        out_specs=(P("slab", None, "mode"), P("slab", "mode")),
        check_vma=False,
    )
```

```python
import jax
import jax.numpy as jnp
from jax import lax
from jax.experimental import pallas as pl
from jax.experimental.pallas import tpu as pltpu
from jax.sharding import PartitionSpec as P

BLK = 64
STRIPS = 16
PARTS = (12, 12)
GROUPS = sum(PARTS)
PER_GROUP = 16
STEPS = 1
SLOTS = 32
HALF = 128
MODES = 256
TWO = 96
REST = HALF - TWO
FLAG_ROWS = 16
TOUCHED_AT = GROUPS * PER_GROUP
MODE_AT = TOUCHED_AT + GROUPS
SHAPES = (1088, MODES)
SHAPES_T = (STRIPS, MODES, 128)
VMEM = pl.BlockSpec(memory_space=pltpu.VMEM)
SUM_WEIGHT = 2 * 10**10
SMEM = pl.BlockSpec(memory_space=pltpu.SMEM)
HBM = pl.BlockSpec(memory_space=pltpu.HBM)


def shape_of(*dims, dtype=jnp.bfloat16):
    return jax.ShapeDtypeStruct(dims, dtype)


def limit(mib):
    return pltpu.CompilerParams(vmem_limit_bytes=mib * 2**20)


def load_kernel(stiff, loaded, sems):
    size = stiff.shape[0] // 8
    copies = [pltpu.make_async_copy(stiff.at[pl.ds(i * size, size)], loaded.at[pl.ds(i * size, size)], sems.at[i])
              for i in range(8)]
    for copy in copies:
        copy.start()
    for copy in copies:
        copy.wait()


def load_stiffness(stiffness):
    return pl.pallas_call(
        load_kernel,
        name="load_stiffness",
        out_shape=shape_of(*stiffness.shape),
        in_specs=[HBM],
        out_specs=VMEM,
        scratch_shapes=[pltpu.SemaphoreType.DMA((8,))],
        compiler_params=limit(24),
        cost_estimate=pl.CostEstimate(flops=0, bytes_accessed=2 * stiffness.size, transcendentals=0),
    )(pltpu.with_memory_space_constraint(stiffness, pltpu.HBM))


def prepare(mode, pieces, shapes, shapes_t):
    for r in range(9):
        rows = jnp.concatenate([piece[:, 128 * r:128 * r + 128] for piece in pieces], 0).T
        if r < 8:
            shapes[128 * r:128 * r + 128, :] = rows
        else:
            shapes[1024:1088, :] = rows[:BLK]
    for k in range(4):
        place = pl.multiple_of(lax.rem(mode + 4 - k, 4) * 64, 64)
        for b in range(STRIPS):
            shapes_t[b, pl.ds(place, 64), :] = pieces[k][:, BLK * b:BLK * b + 128]


def coupling_groups(first, groups, ints, stiff, shapes, shapes_t, slab_row, rest, mode_first):
    low = lax.broadcasted_iota(jnp.int32, (HALF, HALF), 1) < 64

    def one_group(g):
        lefts, images = [], []
        for e in range(PER_GROUP):
            b = ints[(first + g) * PER_GROUP + e]
            x = shapes[pl.ds(pl.multiple_of(b * BLK, BLK), 128), :]
            y = jnp.dot(stiff[(first + g) * PER_GROUP + e], x, preferred_element_type=jnp.float32)
            images.append(y.astype(jnp.bfloat16))
            lefts.append(shapes_t[b])
        c = jnp.dot(jnp.concatenate(lefts, 1), jnp.concatenate(images, 0), preferred_element_type=jnp.float32)
        ref, at = slab_row(g)
        flag = (ints[TOUCHED_AT + first + g] & 1).astype(jnp.float32) + 1.0
        ref[at, TWO:, :] = jnp.full((FLAG_ROWS, HALF), flag, jnp.float32).astype(jnp.bfloat16)
        for t in range(2):
            top, bottom = c[:HALF, 128 * t:128 * t + 128], c[HALF:, 128 * t:128 * t + 128]
            even = jnp.where(low, top, pltpu.roll(bottom, 64, 1)).astype(jnp.bfloat16)
            odd = jnp.where(low, pltpu.roll(top, 64, 1), bottom).astype(jnp.bfloat16)
            if t == 0:
                mode_first[0][g] = even
            else:
                ref[at, :TWO, :] = even[:TWO]
                rest[rest.shape[0] - groups + g] = even[TWO:]
            mode_first[t + 1][g] = odd

    def one_step(j, carry):
        for h in range(groups // STEPS):
            one_group(j * (groups // STEPS) + h)
        return carry

    lax.fori_loop(0, STEPS, one_step, 0)


def slot_of(ints, group):
    return lax.shift_right_logical(ints[TOUCHED_AT + group], 1)


def first_kernel(ints, p0, p3, p2, p1, stiff, rows, rest, own, a, b, shapes, shapes_t):
    prepare(ints[MODE_AT], (p0, p1, p2, p3), shapes, shapes_t)
    coupling_groups(0, PARTS[0], ints, stiff, shapes, shapes_t, lambda g: (rows, g), rest, (own, a, b))


def second_kernel(ints, shapes, shapes_t, stiff, before, rest_before, slab_first, rest, own, a, b):
    rest[:PARTS[0]] = rest_before[...]
    slab_first[...] = jnp.zeros_like(slab_first)
    for g in range(PARTS[0]):
        slab_first[slot_of(ints, g)] = before[g]
    coupling_groups(PARTS[0], PARTS[1], ints, stiff, shapes, shapes_t,
                    lambda g: (slab_first, slot_of(ints, PARTS[0] + g)), rest, (own, a, b))


def coupling_call(kernel, name, groups, rows, rest, args, more_outs=()):
    return pl.pallas_call(
        kernel,
        name=name,
        out_shape=[shape_of(rows, TWO + FLAG_ROWS, HALF), shape_of(rest, REST, HALF)] + [shape_of(groups, HALF, HALF)] * 3
        + [shape_of(*dims) for dims in more_outs],
        in_specs=[SMEM] + [VMEM] * (len(args) - 1),
        out_specs=[VMEM] * (5 + len(more_outs)),
        compiler_params=limit(24),
        cost_estimate=pl.CostEstimate(
            flops=groups * 402653184, bytes_accessed=groups * 2**20, transcendentals=0),
    )(*args)


def sum_of_slabs(got, rows, flag_of):
    sums = [jnp.zeros((rows, HALF), jnp.float32)] * 2
    for s in range(SLOTS):
        block = got[s, :rows, :].astype(jnp.float32)
        sums = [sums[p] + jnp.where(flag_of(s) == p + 1.0, block, 0.0) for p in range(2)]
    return sums


def slab_sum_kernel(got, out, flags):
    for s in range(SLOTS):
        flags[s] = got[s, TWO:, :].astype(jnp.float32)[:8]
    for p, total in enumerate(sum_of_slabs(got, TWO, lambda s: got[s, TWO:, :].astype(jnp.float32)[:1])):
        out[p] = total


def slab_sum(got):
    return pl.pallas_call(
        slab_sum_kernel,
        name="slab_sum",
        out_shape=[shape_of(2, TWO, HALF, dtype=jnp.float32), shape_of(SLOTS, 8, HALF, dtype=jnp.float32)],
        in_specs=[VMEM],
        out_specs=[VMEM] * 2,
        compiler_params=limit(12),
        cost_estimate=pl.CostEstimate(flops=2**22, bytes_accessed=2**21, transcendentals=0),
    )(got)


def mode_sum_kernel(ints, *refs):
    out = refs[-1]
    out[...] = jnp.zeros_like(out)
    for part, groups in enumerate(PARTS):
        for g in range(groups):
            at = sum(PARTS[:part]) + g
            own, a, b = [ref[g].astype(jnp.float32) for ref in refs[3 * part:3 * part + 3]]
            total = own + a + b
            slot = slot_of(ints, at)
            out[slot, :TWO, :] = total[:TWO].astype(jnp.bfloat16)
            out[slot, TWO:, :] = (total[TWO:] + refs[-2][at].astype(jnp.float32)).astype(jnp.bfloat16)


def mode_sum(ints, parts, rest):
    return pl.pallas_call(
        mode_sum_kernel,
        name="mode_sum",
        out_shape=shape_of(SLOTS, HALF, HALF),
        in_specs=[SMEM] + [VMEM] * (3 * len(PARTS) + 1),
        out_specs=VMEM,
        compiler_params=limit(12),
        cost_estimate=pl.CostEstimate(flops=SUM_WEIGHT, bytes_accessed=3 * 2**20, transcendentals=0),
    )(ints, *[array for part in parts for array in part], rest)


def final_kernel(ints, got, flags, tail, coupling, sens):
    row = lax.broadcasted_iota(jnp.int32, (HALF, HALF), 0)
    lane = lax.broadcasted_iota(jnp.int32, (HALF, HALF), 1)
    on_diagonal = jnp.where(lane < 64, row, row + 192) == lane + 64 * ints[MODE_AT]
    for p, total in enumerate(sum_of_slabs(got, HALF, lambda s: flags[s, :1, :])):
        packed = jnp.concatenate([total[:TWO] + tail[p], total[TWO:]], 0)
        columns = packed.T
        coupling[p, :, :HALF] = columns[:64]
        coupling[p, :, HALF:] = columns[64:]
        diagonal = jnp.sum(jnp.where(on_diagonal, packed, 0.0), axis=0, keepdims=True)
        sens[p:p + 1, :] = diagonal[:, :64] + diagonal[:, 64:]


def final_sum(ints, got, flags, tail):
    return pl.pallas_call(
        final_kernel,
        name="final_sum",
        out_shape=(shape_of(2, 64, MODES, dtype=jnp.float32), shape_of(2, 64, dtype=jnp.float32)),
        in_specs=[SMEM] + [VMEM] * 3,
        out_specs=[VMEM] * 2,
        compiler_params=limit(12),
    )(ints, got, flags, tail)


def per_device(mode_shapes, stiffness, elem_block, touched):
    modes = lax.axis_size("mode")
    slabs = lax.axis_size("slab")
    mode = lax.axis_index("mode").astype(jnp.int32)[None]
    around = lambda k: [(i, (i + k) % modes) for i in range(modes)]
    own = mode_shapes.T
    next_own = lax.ppermute(own[:, :HALF], "slab", [(i, i - 1) for i in range(1, slabs)])
    ints = jnp.concatenate([elem_block, touched[0], mode])
    own, ints, next_own = lax.optimization_barrier((jnp.pad(own, ((0, 0), (0, HALF))), ints, next_own))
    own = lax.dynamic_update_slice(own, next_own, (0, own.shape[1] - HALF))
    one, three, two = [lax.ppermute(own, "mode", around(k)) for k in (1, 3, 2)]
    loaded = load_stiffness(stiffness)
    rows, rest, *part_a, shapes, shapes_t = coupling_call(
        first_kernel, "coupling_a", PARTS[0], PARTS[0], PARTS[0], (ints, own, three, two, one, loaded), [SHAPES, SHAPES_T])
    crossed_a = [lax.ppermute(part_a[1], "mode", around(-1)), lax.ppermute(part_a[2], "mode", around(1))]
    slab_first, rest, *part_b = coupling_call(
        second_kernel, "coupling_b", PARTS[1], SLOTS, GROUPS, (ints, shapes, shapes_t, loaded, rows, rest))
    crossed_b = [lax.ppermute(part_b[1], "mode", around(-1)), lax.ppermute(part_b[2], "mode", around(1))]
    rest = lax.ppermute(rest, "mode", around(-2))
    slab_first, crossed_a = lax.optimization_barrier((slab_first, crossed_a))
    got = lax.all_to_all(slab_first, "slab", 0, 0, tiled=True)
    two_away, flags = slab_sum(got)
    tail = lax.ppermute(two_away, "mode", around(-2))
    summed = mode_sum(ints, [part_a[:1] + crossed_a, part_b[:1] + crossed_b], rest)
    later = lax.all_to_all(summed, "slab", 0, 0, tiled=True)
    coupling, sensitivity = final_sum(ints, later, flags, tail)
    return jnp.swapaxes(coupling, 1, 2), sensitivity


def solution(mesh):
    return jax.shard_map(
        per_device,
        mesh=mesh,
        in_specs=(
            P("slab", "mode"),
            P(("slab", "mode"), None, None),
            P(("slab", "mode")),
            P("slab", None),
        ),
        out_specs=(P("slab", None, "mode"), P("slab", "mode")),
        check_vma=False,
    )
```

```python
import jax
import jax.numpy as jnp
from jax import lax
from jax.experimental import pallas as pl
from jax.experimental.pallas import tpu as pltpu
from jax.sharding import PartitionSpec as P

BLK = 64
STRIPS = 16
PARTS = (14, 10)
GROUPS = sum(PARTS)
PER_GROUP = 16
STEPS = 1
SLOTS = 32
HALF = 128
MODES = 256
TWO = 80
REST = HALF - TWO
FLAG_ROWS = 16
TOUCHED_AT = GROUPS * PER_GROUP
MODE_AT = TOUCHED_AT + GROUPS
SHAPES = (1088, MODES)
SHAPES_T = (STRIPS, MODES, 128)
VMEM = pl.BlockSpec(memory_space=pltpu.VMEM)
SUM_WEIGHT = 2 * 10**10
SMEM = pl.BlockSpec(memory_space=pltpu.SMEM)
HBM = pl.BlockSpec(memory_space=pltpu.HBM)


def shape_of(*dims, dtype=jnp.bfloat16):
    return jax.ShapeDtypeStruct(dims, dtype)


def limit(mib):
    return pltpu.CompilerParams(vmem_limit_bytes=mib * 2**20)


def load_kernel(stiff, loaded, sems):
    size = stiff.shape[0] // 8
    copies = [pltpu.make_async_copy(stiff.at[pl.ds(i * size, size)], loaded.at[pl.ds(i * size, size)], sems.at[i])
              for i in range(8)]
    for copy in copies:
        copy.start()
    for copy in copies:
        copy.wait()


def load_stiffness(stiffness):
    return pl.pallas_call(
        load_kernel,
        name="load_stiffness",
        out_shape=shape_of(*stiffness.shape),
        in_specs=[HBM],
        out_specs=VMEM,
        scratch_shapes=[pltpu.SemaphoreType.DMA((8,))],
        compiler_params=limit(24),
        cost_estimate=pl.CostEstimate(flops=0, bytes_accessed=2 * stiffness.size, transcendentals=0),
    )(pltpu.with_memory_space_constraint(stiffness, pltpu.HBM))


def prepare(mode, pieces, shapes, shapes_t):
    for r in range(9):
        rows = jnp.concatenate([piece[:, 128 * r:128 * r + 128] for piece in pieces], 0).T
        if r < 8:
            shapes[128 * r:128 * r + 128, :] = rows
        else:
            shapes[1024:1088, :] = rows[:BLK]
    for k in range(4):
        place = pl.multiple_of(lax.rem(mode + 4 - k, 4) * 64, 64)
        for b in range(STRIPS):
            shapes_t[b, pl.ds(place, 64), :] = pieces[k][:, BLK * b:BLK * b + 128]


def coupling_groups(first, groups, ints, stiff, shapes, shapes_t, slab_row, rest, mode_first):
    low = lax.broadcasted_iota(jnp.int32, (HALF, HALF), 1) < 64

    def one_group(g):
        lefts, images = [], []
        for e in range(PER_GROUP):
            b = ints[(first + g) * PER_GROUP + e]
            x = shapes[pl.ds(pl.multiple_of(b * BLK, BLK), 128), :]
            y = jnp.dot(stiff[(first + g) * PER_GROUP + e], x, preferred_element_type=jnp.float32)
            images.append(y.astype(jnp.bfloat16))
            lefts.append(shapes_t[b])
        c = jnp.dot(jnp.concatenate(lefts, 1), jnp.concatenate(images, 0), preferred_element_type=jnp.float32)
        ref, at = slab_row(g)
        flag = (ints[TOUCHED_AT + first + g] & 1).astype(jnp.float32) + 1.0
        ref[at, TWO:, :] = jnp.full((FLAG_ROWS, HALF), flag, jnp.float32).astype(jnp.bfloat16)
        for t in range(2):
            top, bottom = c[:HALF, 128 * t:128 * t + 128], c[HALF:, 128 * t:128 * t + 128]
            even = jnp.where(low, top, pltpu.roll(bottom, 64, 1)).astype(jnp.bfloat16)
            odd = jnp.where(low, pltpu.roll(top, 64, 1), bottom).astype(jnp.bfloat16)
            if t == 0:
                mode_first[0][g] = even
            else:
                ref[at, :TWO, :] = even[:TWO]
                rest[rest.shape[0] - groups + g] = even[TWO:]
            mode_first[t + 1][g] = odd

    def one_step(j, carry):
        for h in range(groups // STEPS):
            one_group(j * (groups // STEPS) + h)
        return carry

    lax.fori_loop(0, STEPS, one_step, 0)


def slot_of(ints, group):
    return lax.shift_right_logical(ints[TOUCHED_AT + group], 1)


def first_kernel(ints, p0, p3, p2, p1, stiff, rows, rest, own, a, b, shapes, shapes_t):
    prepare(ints[MODE_AT], (p0, p1, p2, p3), shapes, shapes_t)
    coupling_groups(0, PARTS[0], ints, stiff, shapes, shapes_t, lambda g: (rows, g), rest, (own, a, b))


def second_kernel(ints, shapes, shapes_t, stiff, before, rest_before, slab_first, rest, own, a, b):
    rest[:PARTS[0]] = rest_before[...]
    slab_first[...] = jnp.zeros_like(slab_first)
    for g in range(PARTS[0]):
        slab_first[slot_of(ints, g)] = before[g]
    coupling_groups(PARTS[0], PARTS[1], ints, stiff, shapes, shapes_t,
                    lambda g: (slab_first, slot_of(ints, PARTS[0] + g)), rest, (own, a, b))


def coupling_call(kernel, name, groups, rows, rest, args, more_outs=()):
    return pl.pallas_call(
        kernel,
        name=name,
        out_shape=[shape_of(rows, TWO + FLAG_ROWS, HALF), shape_of(rest, REST, HALF)] + [shape_of(groups, HALF, HALF)] * 3
        + [shape_of(*dims) for dims in more_outs],
        in_specs=[SMEM] + [VMEM] * (len(args) - 1),
        out_specs=[VMEM] * (5 + len(more_outs)),
        compiler_params=limit(24),
        cost_estimate=pl.CostEstimate(
            flops=groups * 402653184, bytes_accessed=groups * 2**20, transcendentals=0),
    )(*args)


def sum_of_slabs(got, rows, flag_of):
    sums = [jnp.zeros((rows, HALF), jnp.float32)] * 2
    for s in range(SLOTS):
        block = got[s, :rows, :].astype(jnp.float32)
        sums = [sums[p] + jnp.where(flag_of(s) == p + 1.0, block, 0.0) for p in range(2)]
    return sums


def slab_sum_kernel(got, out, flags):
    for s in range(SLOTS):
        flags[s] = got[s, TWO:, :].astype(jnp.float32)[:8]
    for p, total in enumerate(sum_of_slabs(got, TWO, lambda s: got[s, TWO:, :].astype(jnp.float32)[:1])):
        out[p] = total


def slab_sum(got):
    return pl.pallas_call(
        slab_sum_kernel,
        name="slab_sum",
        out_shape=[shape_of(2, TWO, HALF, dtype=jnp.float32), shape_of(SLOTS, 8, HALF, dtype=jnp.float32)],
        in_specs=[VMEM],
        out_specs=[VMEM] * 2,
        compiler_params=limit(12),
        cost_estimate=pl.CostEstimate(flops=2**22, bytes_accessed=2**21, transcendentals=0),
    )(got)


def mode_sum_kernel(ints, *refs):
    out = refs[-1]
    out[...] = jnp.zeros_like(out)
    for part, groups in enumerate(PARTS):
        for g in range(groups):
            at = sum(PARTS[:part]) + g
            own, a, b = [ref[g].astype(jnp.float32) for ref in refs[3 * part:3 * part + 3]]
            total = own + a + b
            slot = slot_of(ints, at)
            out[slot, :TWO, :] = total[:TWO].astype(jnp.bfloat16)
            out[slot, TWO:, :] = (total[TWO:] + refs[-2][at].astype(jnp.float32)).astype(jnp.bfloat16)


def mode_sum(ints, parts, rest):
    return pl.pallas_call(
        mode_sum_kernel,
        name="mode_sum",
        out_shape=shape_of(SLOTS, HALF, HALF),
        in_specs=[SMEM] + [VMEM] * (3 * len(PARTS) + 1),
        out_specs=VMEM,
        compiler_params=limit(12),
        cost_estimate=pl.CostEstimate(flops=SUM_WEIGHT, bytes_accessed=3 * 2**20, transcendentals=0),
    )(ints, *[array for part in parts for array in part], rest)


def final_kernel(ints, got, flags, tail, coupling, sens):
    row = lax.broadcasted_iota(jnp.int32, (HALF, HALF), 0)
    lane = lax.broadcasted_iota(jnp.int32, (HALF, HALF), 1)
    on_diagonal = jnp.where(lane < 64, row, row + 192) == lane + 64 * ints[MODE_AT]
    for p, total in enumerate(sum_of_slabs(got, HALF, lambda s: flags[s, :1, :])):
        packed = jnp.concatenate([total[:TWO] + tail[p], total[TWO:]], 0)
        columns = packed.T
        coupling[p, :, :HALF] = columns[:64]
        coupling[p, :, HALF:] = columns[64:]
        diagonal = jnp.sum(jnp.where(on_diagonal, packed, 0.0), axis=0, keepdims=True)
        sens[p:p + 1, :] = diagonal[:, :64] + diagonal[:, 64:]


def final_sum(ints, got, flags, tail):
    return pl.pallas_call(
        final_kernel,
        name="final_sum",
        out_shape=(shape_of(2, 64, MODES, dtype=jnp.float32), shape_of(2, 64, dtype=jnp.float32)),
        in_specs=[SMEM] + [VMEM] * 3,
        out_specs=[VMEM] * 2,
        compiler_params=limit(12),
    )(ints, got, flags, tail)


def per_device(mode_shapes, stiffness, elem_block, touched):
    modes = lax.axis_size("mode")
    slabs = lax.axis_size("slab")
    mode = lax.axis_index("mode").astype(jnp.int32)[None]
    around = lambda k: [(i, (i + k) % modes) for i in range(modes)]
    own = mode_shapes.T
    next_own = lax.ppermute(own[:, :HALF], "slab", [(i, i - 1) for i in range(1, slabs)])
    ints = jnp.concatenate([elem_block, touched[0], mode])
    own, ints, next_own = lax.optimization_barrier((jnp.pad(own, ((0, 0), (0, HALF))), ints, next_own))
    own = lax.dynamic_update_slice(own, next_own, (0, own.shape[1] - HALF))
    one, three, two = [lax.ppermute(own, "mode", around(k)) for k in (1, 3, 2)]
    loaded = load_stiffness(stiffness)
    rows, rest, *part_a, shapes, shapes_t = coupling_call(
        first_kernel, "coupling_a", PARTS[0], PARTS[0], PARTS[0], (ints, own, three, two, one, loaded), [SHAPES, SHAPES_T])
    crossed_a = [lax.ppermute(part_a[1], "mode", around(-1)), lax.ppermute(part_a[2], "mode", around(1))]
    slab_first, rest, *part_b = coupling_call(
        second_kernel, "coupling_b", PARTS[1], SLOTS, GROUPS, (ints, shapes, shapes_t, loaded, rows, rest))
    crossed_b = [lax.ppermute(part_b[1], "mode", around(-1)), lax.ppermute(part_b[2], "mode", around(1))]
    rest = lax.ppermute(rest, "mode", around(-2))
    slab_first, crossed_a = lax.optimization_barrier((slab_first, crossed_a))
    got = lax.all_to_all(slab_first, "slab", 0, 0, tiled=True)
    two_away, flags = slab_sum(got)
    tail = lax.ppermute(two_away, "mode", around(-2))
    summed = mode_sum(ints, [part_a[:1] + crossed_a, part_b[:1] + crossed_b], rest)
    later = lax.all_to_all(summed, "slab", 0, 0, tiled=True)
    coupling, sensitivity = final_sum(ints, later, flags, tail)
    return jnp.swapaxes(coupling, 1, 2), sensitivity


def solution(mesh):
    return jax.shard_map(
        per_device,
        mesh=mesh,
        in_specs=(
            P("slab", "mode"),
            P(("slab", "mode"), None, None),
            P(("slab", "mode")),
            P("slab", None),
        ),
        out_specs=(P("slab", None, "mode"), P("slab", "mode")),
        check_vma=False,
    )
```

```python
import jax
import jax.numpy as jnp
from jax import lax
from jax.experimental import pallas as pl
from jax.experimental.pallas import tpu as pltpu
from jax.sharding import PartitionSpec as P

BLK = 64
STRIPS = 16
PARTS = (13, 11)
GROUPS = sum(PARTS)
PER_GROUP = 16
STEPS = 1
SLOTS = 32
HALF = 128
MODES = 256
TWO = 80
REST = HALF - TWO
FLAG_ROWS = 16
TOUCHED_AT = GROUPS * PER_GROUP
MODE_AT = TOUCHED_AT + GROUPS
SHAPES = (1088, MODES)
SHAPES_T = (STRIPS, MODES, 128)
VMEM = pl.BlockSpec(memory_space=pltpu.VMEM)
SUM_WEIGHT = 2 * 10**10
SMEM = pl.BlockSpec(memory_space=pltpu.SMEM)
HBM = pl.BlockSpec(memory_space=pltpu.HBM)


def shape_of(*dims, dtype=jnp.bfloat16):
    return jax.ShapeDtypeStruct(dims, dtype)


def limit(mib):
    return pltpu.CompilerParams(vmem_limit_bytes=mib * 2**20)


def load_kernel(stiff, loaded, sems):
    size = stiff.shape[0] // 8
    copies = [pltpu.make_async_copy(stiff.at[pl.ds(i * size, size)], loaded.at[pl.ds(i * size, size)], sems.at[i])
              for i in range(8)]
    for copy in copies:
        copy.start()
    for copy in copies:
        copy.wait()


def load_stiffness(stiffness):
    return pl.pallas_call(
        load_kernel,
        name="load_stiffness",
        out_shape=shape_of(*stiffness.shape),
        in_specs=[HBM],
        out_specs=VMEM,
        scratch_shapes=[pltpu.SemaphoreType.DMA((8,))],
        compiler_params=limit(24),
        cost_estimate=pl.CostEstimate(flops=0, bytes_accessed=2 * stiffness.size, transcendentals=0),
    )(pltpu.with_memory_space_constraint(stiffness, pltpu.HBM))


def prepare(mode, pieces, shapes, shapes_t):
    for r in range(9):
        rows = jnp.concatenate([piece[:, 128 * r:128 * r + 128] for piece in pieces], 0).T
        if r < 8:
            shapes[128 * r:128 * r + 128, :] = rows
        else:
            shapes[1024:1088, :] = rows[:BLK]
    for k in range(4):
        place = pl.multiple_of(lax.rem(mode + 4 - k, 4) * 64, 64)
        for b in range(STRIPS):
            shapes_t[b, pl.ds(place, 64), :] = pieces[k][:, BLK * b:BLK * b + 128]


def coupling_groups(first, groups, ints, stiff, shapes, shapes_t, slab_row, rest, mode_first):
    low = lax.broadcasted_iota(jnp.int32, (HALF, HALF), 1) < 64

    def one_group(g):
        lefts, images = [], []
        for e in range(PER_GROUP):
            b = ints[(first + g) * PER_GROUP + e]
            x = shapes[pl.ds(pl.multiple_of(b * BLK, BLK), 128), :]
            y = jnp.dot(stiff[(first + g) * PER_GROUP + e], x, preferred_element_type=jnp.float32)
            images.append(y.astype(jnp.bfloat16))
            lefts.append(shapes_t[b])
        c = jnp.dot(jnp.concatenate(lefts, 1), jnp.concatenate(images, 0), preferred_element_type=jnp.float32)
        ref, at = slab_row(g)
        flag = (ints[TOUCHED_AT + first + g] & 1).astype(jnp.float32) + 1.0
        ref[at, TWO:, :] = jnp.full((FLAG_ROWS, HALF), flag, jnp.float32).astype(jnp.bfloat16)
        for t in range(2):
            top, bottom = c[:HALF, 128 * t:128 * t + 128], c[HALF:, 128 * t:128 * t + 128]
            even = jnp.where(low, top, pltpu.roll(bottom, 64, 1)).astype(jnp.bfloat16)
            odd = jnp.where(low, pltpu.roll(top, 64, 1), bottom).astype(jnp.bfloat16)
            if t == 0:
                mode_first[0][g] = even
            else:
                ref[at, :TWO, :] = even[:TWO]
                rest[rest.shape[0] - groups + g] = even[TWO:]
            mode_first[t + 1][g] = odd

    def one_step(j, carry):
        for h in range(groups // STEPS):
            one_group(j * (groups // STEPS) + h)
        return carry

    lax.fori_loop(0, STEPS, one_step, 0)


def slot_of(ints, group):
    return lax.shift_right_logical(ints[TOUCHED_AT + group], 1)


def first_kernel(ints, p0, p3, p2, p1, stiff, rows, rest, own, a, b, shapes, shapes_t):
    prepare(ints[MODE_AT], (p0, p1, p2, p3), shapes, shapes_t)
    coupling_groups(0, PARTS[0], ints, stiff, shapes, shapes_t, lambda g: (rows, g), rest, (own, a, b))


def second_kernel(ints, shapes, shapes_t, stiff, before, rest_before, slab_first, rest, own, a, b):
    rest[:PARTS[0]] = rest_before[...]
    slab_first[...] = jnp.zeros_like(slab_first)
    for g in range(PARTS[0]):
        slab_first[slot_of(ints, g)] = before[g]
    coupling_groups(PARTS[0], PARTS[1], ints, stiff, shapes, shapes_t,
                    lambda g: (slab_first, slot_of(ints, PARTS[0] + g)), rest, (own, a, b))


def coupling_call(kernel, name, groups, rows, rest, args, more_outs=()):
    return pl.pallas_call(
        kernel,
        name=name,
        out_shape=[shape_of(rows, TWO + FLAG_ROWS, HALF), shape_of(rest, REST, HALF)] + [shape_of(groups, HALF, HALF)] * 3
        + [shape_of(*dims) for dims in more_outs],
        in_specs=[SMEM] + [VMEM] * (len(args) - 1),
        out_specs=[VMEM] * (5 + len(more_outs)),
        compiler_params=limit(24),
        cost_estimate=pl.CostEstimate(
            flops=groups * 402653184, bytes_accessed=groups * 2**20, transcendentals=0),
    )(*args)


def sum_of_slabs(got, rows, flag_of):
    sums = [jnp.zeros((rows, HALF), jnp.float32)] * 2
    for s in range(SLOTS):
        block = got[s, :rows, :].astype(jnp.float32)
        sums = [sums[p] + jnp.where(flag_of(s) == p + 1.0, block, 0.0) for p in range(2)]
    return sums


def slab_sum_kernel(got, out, flags):
    for s in range(SLOTS):
        flags[s] = got[s, TWO:, :].astype(jnp.float32)[:8]
    for p, total in enumerate(sum_of_slabs(got, TWO, lambda s: got[s, TWO:, :].astype(jnp.float32)[:1])):
        out[p] = total


def slab_sum(got):
    return pl.pallas_call(
        slab_sum_kernel,
        name="slab_sum",
        out_shape=[shape_of(2, TWO, HALF, dtype=jnp.float32), shape_of(SLOTS, 8, HALF, dtype=jnp.float32)],
        in_specs=[VMEM],
        out_specs=[VMEM] * 2,
        compiler_params=limit(12),
        cost_estimate=pl.CostEstimate(flops=2**22, bytes_accessed=2**21, transcendentals=0),
    )(got)


def mode_sum_kernel(ints, *refs):
    out = refs[-1]
    out[...] = jnp.zeros_like(out)
    for part, groups in enumerate(PARTS):
        for g in range(groups):
            at = sum(PARTS[:part]) + g
            own, a, b = [ref[g].astype(jnp.float32) for ref in refs[3 * part:3 * part + 3]]
            total = own + a + b
            slot = slot_of(ints, at)
            out[slot, :TWO, :] = total[:TWO].astype(jnp.bfloat16)
            out[slot, TWO:, :] = (total[TWO:] + refs[-2][at].astype(jnp.float32)).astype(jnp.bfloat16)


def mode_sum(ints, parts, rest):
    return pl.pallas_call(
        mode_sum_kernel,
        name="mode_sum",
        out_shape=shape_of(SLOTS, HALF, HALF),
        in_specs=[SMEM] + [VMEM] * (3 * len(PARTS) + 1),
        out_specs=VMEM,
        compiler_params=limit(12),
        cost_estimate=pl.CostEstimate(flops=SUM_WEIGHT, bytes_accessed=3 * 2**20, transcendentals=0),
    )(ints, *[array for part in parts for array in part], rest)


def final_kernel(ints, got, flags, tail, coupling, sens):
    row = lax.broadcasted_iota(jnp.int32, (HALF, HALF), 0)
    lane = lax.broadcasted_iota(jnp.int32, (HALF, HALF), 1)
    on_diagonal = jnp.where(lane < 64, row, row + 192) == lane + 64 * ints[MODE_AT]
    for p, total in enumerate(sum_of_slabs(got, HALF, lambda s: flags[s, :1, :])):
        packed = jnp.concatenate([total[:TWO] + tail[p], total[TWO:]], 0)
        columns = packed.T
        coupling[p, :, :HALF] = columns[:64]
        coupling[p, :, HALF:] = columns[64:]
        diagonal = jnp.sum(jnp.where(on_diagonal, packed, 0.0), axis=0, keepdims=True)
        sens[p:p + 1, :] = diagonal[:, :64] + diagonal[:, 64:]


def final_sum(ints, got, flags, tail):
    return pl.pallas_call(
        final_kernel,
        name="final_sum",
        out_shape=(shape_of(2, 64, MODES, dtype=jnp.float32), shape_of(2, 64, dtype=jnp.float32)),
        in_specs=[SMEM] + [VMEM] * 3,
        out_specs=[VMEM] * 2,
        compiler_params=limit(12),
    )(ints, got, flags, tail)


def per_device(mode_shapes, stiffness, elem_block, touched):
    modes = lax.axis_size("mode")
    slabs = lax.axis_size("slab")
    mode = lax.axis_index("mode").astype(jnp.int32)[None]
    around = lambda k: [(i, (i + k) % modes) for i in range(modes)]
    own = mode_shapes.T
    next_own = lax.ppermute(own[:, :HALF], "slab", [(i, i - 1) for i in range(1, slabs)])
    ints = jnp.concatenate([elem_block, touched[0], mode])
    own, ints, next_own = lax.optimization_barrier((jnp.pad(own, ((0, 0), (0, HALF))), ints, next_own))
    own = lax.dynamic_update_slice(own, next_own, (0, own.shape[1] - HALF))
    one, three, two = [lax.ppermute(own, "mode", around(k)) for k in (1, 3, 2)]
    loaded = load_stiffness(stiffness)
    rows, rest, *part_a, shapes, shapes_t = coupling_call(
        first_kernel, "coupling_a", PARTS[0], PARTS[0], PARTS[0], (ints, own, three, two, one, loaded), [SHAPES, SHAPES_T])
    crossed_a = [lax.ppermute(part_a[1], "mode", around(-1)), lax.ppermute(part_a[2], "mode", around(1))]
    slab_first, rest, *part_b = coupling_call(
        second_kernel, "coupling_b", PARTS[1], SLOTS, GROUPS, (ints, shapes, shapes_t, loaded, rows, rest))
    crossed_b = [lax.ppermute(part_b[1], "mode", around(-1)), lax.ppermute(part_b[2], "mode", around(1))]
    rest = lax.ppermute(rest, "mode", around(-2))
    slab_first, crossed_a = lax.optimization_barrier((slab_first, crossed_a))
    got = lax.all_to_all(slab_first, "slab", 0, 0, tiled=True)
    two_away, flags = slab_sum(got)
    tail = lax.ppermute(two_away, "mode", around(-2))
    summed = mode_sum(ints, [part_a[:1] + crossed_a, part_b[:1] + crossed_b], rest)
    later = lax.all_to_all(summed, "slab", 0, 0, tiled=True)
    coupling, sensitivity = final_sum(ints, later, flags, tail)
    return jnp.swapaxes(coupling, 1, 2), sensitivity


def solution(mesh):
    return jax.shard_map(
        per_device,
        mesh=mesh,
        in_specs=(
            P("slab", "mode"),
            P(("slab", "mode"), None, None),
            P(("slab", "mode")),
            P("slab", None),
        ),
        out_specs=(P("slab", None, "mode"), P("slab", "mode")),
        check_vma=False,
    )
```
